32 devices in a mesh: mode: 4 (over z), tile: 8 (over y, x, core).
Axes of the slice: x: 2, y: 2, z: 4, core: 2. Of those that a mesh axis runs over, the one named last changes fastest.
Arguments:
- distribution: float32 [4096, 64, 128], P('mode', 'tile'), may hold values from -6 to 6
- courant: float32 [2, 4096], P(None, 'mode'), may hold values from -0.4 to 0.4
- relax_rate: float32 [4096], P('mode'), may hold values from 0.1 to 2
- scatter_weight: float32 [4096, 4096], P('mode'), may hold values from -0.09375 to 0.09375
- cell_flags: int32 [64, 128], P('tile'), may hold values 0 or 1
Outputs:
- evolved: float32 [4096, 64, 128], P('mode', 'tile')
The draws below stay inside these ranges and needn't reach their ends.
All inputs are finite; a program needn't handle non-finite values. No bound on the sum of `cell_flags` on one device may be relied on, other than what follows from the above.
Results may differ from the reference program's by a relative error of at most 0.0012.
Values may be sent and summed in bfloat16 or wider, within the bound.
No kernel may reach another device: no remote copies, remote signals or barrier semaphores. Data moves between devices by JAX's collectives and lax.ppermute only.
A program may use at most 128 MiB of HBM per device.

```python
import math
import jax
import jax.numpy as jnp
from jax import lax

MODES = 4096
NY = 128
NX = 64


def set_ends(entries, key, least, largest):
    spot = [jax.random.randint(jax.random.fold_in(key, axis), (), 0, length) for axis, length in enumerate(entries.shape)]
    longest = entries.shape.index(max(entries.shape))
    beside = spot[:longest] + [(spot[longest] + 1) % entries.shape[longest]] + spot[longest + 1:]
    return entries.at[tuple(spot)].set(least).at[tuple(beside)].set(largest)


def level_of(key, shape, cuts, low, high):
    level = 1.0
    for axis_at, shards_of in cuts:
        heights = jax.random.uniform(jax.random.fold_in(jax.random.fold_in(key, 6), axis_at), (shards_of,), jnp.float32, low / len(cuts), high / len(cuts))
        level = level * jnp.repeat(jnp.exp(heights), shape[axis_at] // shards_of).reshape((-1,) + (1,) * (len(shape) - 1 - axis_at))
    return level


def bell_draw(own_key, extent, scale, most, split=(), kind=jnp.bfloat16):
    level = level_of(own_key, extent, split, -0.22, 0.18) if split else 1.0
    entries = jax.random.normal(own_key, extent, jnp.float32) * scale * level
    return jnp.minimum(jnp.maximum(entries, -most), most).astype(kind)


def setup_inputs(seed: int = 0) -> dict:
    streams_of = jax.random.split(jax.random.key(seed), 6)
    return {
        "distribution": bell_draw(streams_of[0], (MODES, NX, NY), 1.0, 6.0, ((0, 4), (1, 8)), jnp.float32),
        "courant": jnp.clip(jax.random.uniform(streams_of[1], (2, MODES), jnp.float32, -0.4, 0.4) * level_of(streams_of[1], (2, MODES), ((1, 4),), -0.4, 0.0), -0.4, 0.4),
        "relax_rate": jnp.clip(jnp.exp(math.log(2.0) - 2.9957323 * jax.random.uniform(streams_of[2], (MODES,), jnp.float32) ** level_of(streams_of[2], (MODES,), ((0, 4),), -0.2, 0.2)), 0.1, 2.0),
        "scatter_weight": bell_draw(streams_of[3], (MODES, MODES), MODES ** -0.5, 0.09375, ((0, 4),), jnp.float32),
        "cell_flags": set_ends((jax.random.randint(streams_of[4], (NX, NY), 0, 4) < 1).astype(jnp.int32), jax.random.fold_in(streams_of[4], 1), 0, 1),
    }


time_step = 0.25
wall_rate = 2.0


def transport_rows(padded, cx, cy):
    full = jnp.pad(padded, ((0, 0), (0, 0), (2, 2)))
    centre = full[:, 2:-2, 2:-2]
    back_x = 1.5 * centre - 2.0 * full[:, 1:-3, 2:-2] + 0.5 * full[:, :-4, 2:-2]
    fwd_x = -1.5 * centre + 2.0 * full[:, 3:-1, 2:-2] - 0.5 * full[:, 4:, 2:-2]
    back_y = 1.5 * centre - 2.0 * full[:, 2:-2, 1:-3] + 0.5 * full[:, 2:-2, :-4]
    fwd_y = -1.5 * centre + 2.0 * full[:, 2:-2, 3:-1] - 0.5 * full[:, 2:-2, 4:]
    return (jnp.maximum(cx, 0.0) * back_x + jnp.minimum(cx, 0.0) * fwd_x
            + jnp.maximum(cy, 0.0) * back_y + jnp.minimum(cy, 0.0) * fwd_y)


def advance(field, courant, relax_rate, scatter_weight, flags):
    cx = courant[0][:, None, None]
    cy = courant[1][:, None, None]
    padded = jnp.pad(field, ((0, 0), (2, 2), (0, 0)))
    moved = transport_rows(padded, cx, cy)
    rounded = field.astype(jnp.bfloat16).reshape(field.shape[0], -1).astype(jnp.float32)
    gain = jnp.dot(scatter_weight, rounded, precision=lax.Precision.HIGHEST,
                   preferred_element_type=jnp.float32).reshape(field.shape)
    rate = relax_rate[:, None, None]
    return field - moved + time_step * (gain - rate * field - wall_rate * flags * field)


def reference(distribution, courant, relax_rate, scatter_weight, cell_flags):
    flags = cell_flags.astype(jnp.float32)[None]
    first = advance(distribution, courant, relax_rate, scatter_weight, flags)
    return advance(first, courant, relax_rate, scatter_weight, flags)
```

```python
import functools

import jax
import jax.numpy as jnp
from jax import lax
from jax.experimental import pallas as pl
from jax.experimental.pallas import tpu as pltpu
from jax.sharding import PartitionSpec as P

time_step = 0.25
wall_rate = 2.0
chunk_rows = 4
bf16 = jnp.bfloat16
f32 = jnp.float32


def pack_kernel(rows, modes, field_ref, rounded_ref, low_ref, high_ref):
    for r in range(rows):
        line = field_ref[pl.ds(r, modes, stride=rows), :]
        rounded_ref[r] = line.astype(bf16)
        if r < 2:
            low_ref[r] = line
        if r >= rows - 2:
            high_ref[r - rows + 2] = line


def pack(field):
    modes, rows, columns = field.shape
    block = 256
    return pl.pallas_call(
        functools.partial(pack_kernel, rows, block),
        grid=(modes // block,),
        in_specs=[pl.BlockSpec((block * rows, columns), lambda i: (i, 0))],
        out_specs=[
            pl.BlockSpec((rows, block, columns), lambda i: (0, i, 0)),
            pl.BlockSpec((2, block, columns), lambda i: (0, i, 0)),
            pl.BlockSpec((2, block, columns), lambda i: (0, i, 0)),
        ],
        out_shape=[
            jax.ShapeDtypeStruct((rows, modes, columns), bf16),
            jax.ShapeDtypeStruct((2, modes, columns), f32),
            jax.ShapeDtypeStruct((2, modes, columns), f32),
        ],
        cost_estimate=pl.CostEstimate(flops=1000, bytes_accessed= 1000, transcendentals=0),
        compiler_params=pltpu.CompilerParams(vmem_limit_bytes=32 * 2**20),
        name="pack",
    )(field.reshape(modes * rows, columns))


def local_line(lines, r, params, flags):
    cx, cy, rate = params
    centre = lines(r)
    shape = centre.shape
    lane = lax.broadcasted_iota(jnp.int32, shape, 1)
    columns = shape[1]

    def moved(by):
        turned = pltpu.roll(centre, by % columns, 1)
        keep = lane >= by if by > 0 else lane < columns + by
        return jnp.where(keep, turned, 0.0)

    back_x = 1.5 * centre - 2.0 * lines(r - 1) + 0.5 * lines(r - 2)
    fwd_x = -1.5 * centre + 2.0 * lines(r + 1) - 0.5 * lines(r + 2)
    back_y = 1.5 * centre - 2.0 * moved(1) + 0.5 * moved(2)
    fwd_y = -1.5 * centre + 2.0 * moved(-1) - 0.5 * moved(-2)
    transport = (
        jnp.maximum(cx, 0.0) * back_x
        + jnp.minimum(cx, 0.0) * fwd_x
        + jnp.maximum(cy, 0.0) * back_y
        + jnp.minimum(cy, 0.0) * fwd_y
    )
    return centre - transport - time_step * (rate * centre + wall_rate * flags * centre)


def base_kernel(rows, modes, strided, field_ref, before_ref, after_ref, cx_ref, cy_ref, rate_ref, flags_ref, out_ref):
    params = (cx_ref[...], cy_ref[...], rate_ref[...])

    def lines(r):
        if r < 0:
            return before_ref[r + 2]
        if r >= rows:
            return after_ref[r - rows]
        if strided:
            return field_ref[pl.ds(r, modes, stride=rows), :]
        return field_ref[r]

    for r in range(rows):
        out_ref[r] = local_line(lines, r, params, flags_ref[r:r + 1, :])


def base(field, before, after, params, flags, strided):
    rows, columns = flags.shape
    modes = before.shape[1]
    block = 128
    if strided:
        field_spec = pl.BlockSpec((block * rows, columns), lambda i: (i, 0))
        field = field.reshape(modes * rows, columns)
    else:
        field_spec = pl.BlockSpec((rows, block, columns), lambda i: (0, i, 0))
    side = pl.BlockSpec((2, block, columns), lambda i: (0, i, 0))
    per_mode = pl.BlockSpec((block, 1), lambda i: (i, 0))
    return pl.pallas_call(
        functools.partial(base_kernel, rows, block, strided),
        grid=(modes // block,),
        in_specs=[field_spec, side, side, per_mode, per_mode, per_mode, pl.BlockSpec((rows, columns), lambda i: (0, 0))],
        out_specs=pl.BlockSpec((rows, block, columns), lambda i: (0, i, 0)),
        out_shape=jax.ShapeDtypeStruct((rows, modes, columns), f32),
        cost_estimate=pl.CostEstimate(flops=1000, bytes_accessed= 1000, transcendentals=0),
        compiler_params=pltpu.CompilerParams(vmem_limit_bytes=32 * 2**20),
        name="base",
    )(field, before, after, *params, flags)


def gains_kernel(own_steps, order_ref, own_w_ref, edge_w_ref, a_ref, b_ref, c_ref, d_ref, base_ref, first_ref, rounded_ref, sum_ref, cells_ref):
    rows, depth, lanes = a_ref.shape

    @pl.when(pl.program_id(0) == 0)
    def _():
        for j, part in enumerate((a_ref, b_ref, c_ref, d_ref)):
            at = pl.ds(pl.multiple_of(order_ref[j] * depth, depth), depth)
            for r in range(rows):
                cells_ref[at, r * lanes:(r + 1) * lanes] = part[r]

    @pl.when(pl.program_id(0) < own_steps)
    def _():
        total = jnp.dot(own_w_ref[...], cells_ref[...], preferred_element_type=f32)
        for r in range(rows):
            line = base_ref[r] + time_step * total[:, r * lanes:(r + 1) * lanes]
            first_ref[r] = line
            rounded_ref[r] = line.astype(bf16)

    @pl.when(pl.program_id(0) >= own_steps)
    def _():
        at = pl.ds(pl.multiple_of(order_ref[4] * depth, depth), 3 * depth)
        total = jnp.dot(edge_w_ref[...], cells_ref[at, :], preferred_element_type=f32)
        for r in range(rows):
            sum_ref[r] = total[:, r * lanes:(r + 1) * lanes].astype(bf16)


def gains(order, own_w, edge_w, parts, based, at):
    modes, depth = own_w.shape
    rows, _, columns = parts[0].shape
    block = modes // 2
    steps = modes // block
    first = lambda i, order: (0, jnp.minimum(i, steps - 1), 0)
    second = lambda i, order: (0, jnp.maximum(i - steps, 0), 0)
    whole = pl.BlockSpec(parts[0].shape, lambda i, order: (0, 0, 0))
    return pl.pallas_call(
        functools.partial(gains_kernel, steps),
        grid_spec=pltpu.PrefetchScalarGridSpec(
            num_scalar_prefetch=1,
            grid=(2 * steps,),
            in_specs=[
                pl.BlockSpec((block, depth), lambda i, order: (jnp.minimum(i, steps - 1), 0)),
                pl.BlockSpec((block, depth - modes), lambda i, order: (jnp.maximum(i - steps, 0), 0)),
                whole, whole, whole, whole,
                pl.BlockSpec((rows, block, columns), lambda i, order: (at, jnp.minimum(i, steps - 1), 0)),
            ],
            out_specs=[
                pl.BlockSpec((rows, block, columns), first),
                pl.BlockSpec((rows, block, columns), first),
                pl.BlockSpec((rows, block, columns), second),
            ],
            scratch_shapes=[pltpu.VMEM((depth, rows * columns), bf16)],
        ),
        out_shape=[
            jax.ShapeDtypeStruct((rows, modes, columns), f32),
            jax.ShapeDtypeStruct((rows, modes, columns), bf16),
            jax.ShapeDtypeStruct((rows, modes, columns), bf16),
        ],
        cost_estimate=pl.CostEstimate(flops=1000, bytes_accessed= 1000, transcendentals=0),
        compiler_params=pltpu.CompilerParams(vmem_limit_bytes=44 * 2**20),
        name="gains",
    )(order, own_w, edge_w, *parts, based)


def unpack_kernel(rows, modes, each, *refs):
    out_ref = refs[-1]
    count = len(refs) // 2
    for r in range(rows):
        line = refs[r // each][r % each] + time_step * refs[count + r // each][r % each].astype(f32)
        out_ref[pl.ds(r, modes, stride=rows), :] = line


def unpack(firsts, sums):
    each, modes, columns = firsts[0].shape
    rows = each * len(firsts)
    block = 256
    flat = pl.pallas_call(
        functools.partial(unpack_kernel, rows, block, each),
        grid=(modes // block,),
        in_specs=[pl.BlockSpec((each, block, columns), lambda i: (0, i, 0))] * (2 * len(firsts)),
        out_specs=pl.BlockSpec((block * rows, columns), lambda i: (i, 0)),
        out_shape=jax.ShapeDtypeStruct((modes * rows, columns), f32),
        cost_estimate=pl.CostEstimate(flops=1000, bytes_accessed= 1000, transcendentals=0),
        compiler_params=pltpu.CompilerParams(vmem_limit_bytes=32 * 2**20),
        name="unpack",
    )(*firsts, *sums)
    return flat.reshape(modes, rows, columns)


inward = [(0, 1), (3, 2)]
outward = [(1, 0), (2, 3)]
across = [(1, 2), (2, 1)]


def line_of_four(distribution, courant, relax_rate, scatter_weight, cell_flags):
    modes, rows, columns = distribution.shape
    plane = lax.axis_index("mode")
    beside = plane + 1 - 2 * (plane % 2)
    order = jnp.stack([plane, beside, 3 - plane, 3 - beside, (plane < 2).astype(jnp.int32)])
    flags = cell_flags.astype(f32)
    params = tuple(v[:, None] for v in (courant[0], courant[1], relax_rate))
    count = lax.axis_size("tile")
    up = [(i, i + 1) for i in range(count - 1)]
    down = [(i + 1, i) for i in range(count - 1)]
    send = functools.partial(lax.ppermute, axis_name="mode")
    after = lambda value, *earlier: lax.optimization_barrier((value, *earlier))[0]

    rounded, low, high = pack(distribution)
    x1, x2 = rounded[:chunk_rows], rounded[chunk_rows:]

    share = modes // count
    piece = lax.dynamic_slice(
        scatter_weight,
        (lax.axis_index("tile") * share, jnp.where(plane == 0, modes, 0)),
        (share, 3 * modes),
    )
    piece = send(after(piece.astype(bf16), rounded), perm=inward)
    own_w = after(scatter_weight, rounded).astype(bf16)
    b1 = send(x1, perm=across)
    edge_w = lax.all_gather(after(piece, own_w, b1), "tile", axis=0, tiled=True)
    b2 = send(after(x2, b1), perm=across)
    a1 = send(after(x1, piece), perm=inward)
    a2 = send(after(x2, a1), perm=inward)
    c1 = send(a1, perm=across)
    c2 = send(a2, perm=across)
    based = base(
        distribution,
        lax.ppermute(high, "tile", up),
        lax.ppermute(low, "tile", down),
        params, flags, True,
    )
    first1, own1, sum1 = gains(order, own_w, edge_w, (x1, a1, b1, c1), based, 0)
    first2, own2, sum2 = gains(order, own_w, edge_w, (x2, a2, b2, c2), based, 1)
    b1 = send(own1, perm=across)
    b2 = send(after(own2, b1), perm=across)
    field1 = first1 + time_step * send(sum1, perm=outward).astype(f32)
    x1 = field1.astype(bf16)
    a1 = send(x1, perm=inward)
    field2 = first2 + time_step * send(sum2, perm=outward).astype(f32)
    x2 = field2.astype(bf16)
    a2 = send(x2, perm=inward)
    c1 = send(a1, perm=across)
    c2 = send(a2, perm=across)
    based = base(
        jnp.concatenate([field1, field2], axis=0),
        lax.ppermute(field2[-2:], "tile", up),
        lax.ppermute(field1[:2], "tile", down),
        params, flags, False,
    )
    first1, _, sum1 = gains(order, own_w, edge_w, (x1, a1, b1, c1), based, 0)
    first2, _, sum2 = gains(order, own_w, edge_w, (x2, a2, b2, c2), based, 1)
    return unpack([first1, first2], [send(sum1, perm=outward), send(sum2, perm=outward)])


def extended(block, width):
    count = lax.axis_size("tile")
    up = [(i, i + 1) for i in range(count - 1)]
    down = [(i + 1, i) for i in range(count - 1)]
    low = lax.ppermute(block[:, -width:], "tile", up)
    high = lax.ppermute(block[:, :width], "tile", down)
    return jnp.concatenate([low, block, high], axis=1)


def gathered(distribution, courant, relax_rate, scatter_weight, cell_flags):
    cx = courant[0][:, None, None]
    cy = courant[1][:, None, None]
    rate = relax_rate[:, None, None]
    flags = cell_flags.astype(f32)[None]
    weight = scatter_weight.astype(bf16)
    field = distribution
    for step in range(2):
        full = jnp.pad(extended(field, 2), ((0, 0), (0, 0), (2, 2)))
        centre = full[:, 2:-2, 2:-2]
        back_x = 1.5 * centre - 2.0 * full[:, 1:-3, 2:-2] + 0.5 * full[:, :-4, 2:-2]
        fwd_x = -1.5 * centre + 2.0 * full[:, 3:-1, 2:-2] - 0.5 * full[:, 4:, 2:-2]
        back_y = 1.5 * centre - 2.0 * full[:, 2:-2, 1:-3] + 0.5 * full[:, 2:-2, :-4]
        fwd_y = -1.5 * centre + 2.0 * full[:, 2:-2, 3:-1] - 0.5 * full[:, 2:-2, 4:]
        transport = (
            jnp.maximum(cx, 0.0) * back_x
            + jnp.minimum(cx, 0.0) * fwd_x
            + jnp.maximum(cy, 0.0) * back_y
            + jnp.minimum(cy, 0.0) * fwd_y
        )
        flat = field.astype(bf16).reshape(field.shape[0], -1)
        flat = lax.all_gather(flat, "mode", axis=0, tiled=True)
        gain = jnp.dot(weight, flat, preferred_element_type=f32).reshape(field.shape)
        field = field - transport + time_step * (gain - rate * field - wall_rate * flags * field)
    return field


def body(*args):
    if lax.axis_size("mode") == 4 and args[0].shape[1] == 2 * chunk_rows:
        return line_of_four(*args)
    return gathered(*args)


def solution(mesh):
    in_specs = (
        P("mode", "tile", None),
        P(None, "mode"),
        P("mode"),
        P("mode", None),
        P("tile", None),
    )
    out_specs = P("mode", "tile", None)
    return jax.shard_map(body, mesh=mesh, in_specs=in_specs, out_specs=out_specs, check_vma=False)
```

```python
import functools

import jax
import jax.numpy as jnp
from jax import lax
from jax.experimental import pallas as pl
from jax.experimental.pallas import tpu as pltpu
from jax.sharding import PartitionSpec as P

time_step = 0.25
wall_rate = 2.0
bf16 = jnp.bfloat16
f32 = jnp.float32


def small(limit):
    return dict(
        cost_estimate=pl.CostEstimate(flops=1000, bytes_accessed=1000, transcendentals=0),
        compiler_params=pltpu.CompilerParams(vmem_limit_bytes=limit * 2**20),
    )


def pack_kernel(blocks, field_ref, one_ref, two_ref, low_ref, high_ref, held_ref, done_ref):
    modes, cells = one_ref.shape
    columns = field_ref.shape[1]
    half = cells // columns
    rows = 2 * half
    block = modes // blocks
    copies = []
    for i in range(blocks):
        at = pl.ds(i * block * rows, block * rows)
        copies.append(pltpu.make_async_copy(field_ref.at[at], held_ref.at[at], done_ref.at[i]))
        copies[i].start()
    for i in range(blocks):
        copies[i].wait()
        to = slice(i * block, (i + 1) * block)
        for r in range(rows):
            line = held_ref[pl.ds(i * block * rows + r, block, stride=rows), :]
            to_ref = one_ref if r < half else two_ref
            to_ref[to, r % half * columns:(r % half + 1) * columns] = line.astype(bf16)
            if r < 2:
                low_ref[to, r * columns:(r + 1) * columns] = line
            if r >= rows - 2:
                at = r - rows + 2
                high_ref[to, at * columns:(at + 1) * columns] = line


def pack(field):
    modes, rows, columns = field.shape
    blocks = 4
    shape = lambda count, kind: jax.ShapeDtypeStruct((modes, count * columns), kind)
    return pl.pallas_call(
        functools.partial(pack_kernel, blocks),
        in_specs=[pl.BlockSpec(memory_space=pl.ANY)],
        out_specs=[pl.BlockSpec(memory_space=pltpu.VMEM)] * 4,
        out_shape=[shape(rows // 2, bf16)] * 2 + [shape(2, f32)] * 2,
        scratch_shapes=[pltpu.VMEM((modes * rows, columns), f32), pltpu.SemaphoreType.DMA((blocks,))],
        name="pack",
        **small(46),
    )(field.reshape(modes * rows, columns))


def local_line(lines, r, params, flags):
    cx, cy, rate = params
    centre = lines(r)
    lane = lax.broadcasted_iota(jnp.int32, centre.shape, 1)
    columns = centre.shape[1]

    def moved(by):
        turned = pltpu.roll(centre, by % columns, 1)
        keep = lane >= by if by > 0 else lane < columns + by
        return jnp.where(keep, turned, 0.0)

    back_x = 1.5 * centre - 2.0 * lines(r - 1) + 0.5 * lines(r - 2)
    fwd_x = -1.5 * centre + 2.0 * lines(r + 1) - 0.5 * lines(r + 2)
    back_y = 1.5 * centre - 2.0 * moved(1) + 0.5 * moved(2)
    fwd_y = -1.5 * centre + 2.0 * moved(-1) - 0.5 * moved(-2)
    transport = (
        jnp.maximum(cx, 0.0) * back_x
        + jnp.minimum(cx, 0.0) * fwd_x
        + jnp.maximum(cy, 0.0) * back_y
        + jnp.minimum(cy, 0.0) * fwd_y
    )
    return centre - transport - time_step * (rate * centre + wall_rate * flags * centre)


def column(line):
    count = line.shape[1]
    at = lax.broadcasted_iota(jnp.int32, (count, count), 0)
    lane = lax.broadcasted_iota(jnp.int32, (count, count), 1)
    return jnp.sum(jnp.where(at == lane, line, 0.0), axis=1, keepdims=True)


def base_kernel(rows, modes, strided, *refs):
    *field_refs, before_ref, behind_ref, courant_ref, rate_ref, flags_ref, one_ref, two_ref = refs
    params = (column(courant_ref[0:1, :]), column(courant_ref[1:2, :]), column(rate_ref[...]))
    flags = flags_ref[...].astype(f32)
    columns = flags_ref.shape[1]
    half = rows // 2
    cut = lambda at: slice(at * columns, (at + 1) * columns)

    def lines(r):
        if r < 0:
            return before_ref[:, cut(r + 2)]
        if r >= rows:
            return behind_ref[:, cut(r - rows)]
        if strided:
            return field_refs[0][pl.ds(r, modes, stride=rows), :]
        return field_refs[r // half][:, cut(r % half)]

    for r in range(rows):
        to_ref = one_ref if r < half else two_ref
        to_ref[:, cut(r % half)] = local_line(lines, r, params, flags[r:r + 1, :])


def base(fields, before, behind, courant, rate, flags):
    rows, columns = flags.shape
    modes = before.shape[0]
    block = 128
    spec = lambda count: pl.BlockSpec((block, count * columns), lambda i: (i, 0))
    strided = len(fields) == 1
    if strided:
        field_specs = [pl.BlockSpec((block * rows, columns), lambda i: (i, 0))]
        fields = [fields[0].reshape(modes * rows, columns)]
    else:
        field_specs = [spec(rows // 2)] * 2
    per_mode = lambda count: pl.BlockSpec((count, block), lambda i: (0, i))
    return pl.pallas_call(
        functools.partial(base_kernel, rows, block, strided),
        grid=(modes // block,),
        in_specs=field_specs + [spec(2), spec(2), per_mode(2), per_mode(1), pl.BlockSpec((rows, columns), lambda i: (0, 0))],
        out_specs=[spec(rows // 2)] * 2,
        out_shape=[jax.ShapeDtypeStruct((modes, rows // 2 * columns), f32)] * 2,
        name="base",
        **small(12),
    )(*fields, before, behind, courant, rate.reshape(1, modes), flags)


def piece_kernel(w_ref, out_ref, held_ref, done_ref):
    share, kept = out_ref.shape
    at = pl.multiple_of(lax.axis_index("tile") * share, share)
    skipped = w_ref.shape[1] - kept
    left = pl.multiple_of(jnp.where(lax.axis_index("mode") == 0, skipped, 0), skipped)
    copy = pltpu.make_async_copy(w_ref.at[pl.ds(at, share), pl.ds(left, kept)], held_ref, done_ref)
    copy.start()
    copy.wait()
    out_ref[...] = held_ref[...].astype(bf16)


def piece_of(weights, count):
    modes, depth = weights.shape
    shape = (modes // count, depth - modes)
    return pl.pallas_call(
        piece_kernel,
        in_specs=[pl.BlockSpec(memory_space=pl.ANY)],
        out_specs=pl.BlockSpec(memory_space=pltpu.VMEM),
        out_shape=jax.ShapeDtypeStruct(shape, bf16),
        scratch_shapes=[pltpu.VMEM(shape, f32), pltpu.SemaphoreType.DMA],
        name="piece",
        **small(56),
    )(weights)


def meet_kernel(low, first_ref, sum_ref, field_ref, one_ref, two_ref, side_ref):
    block = 128
    half = one_ref.shape[1]
    side = side_ref.shape[1]

    def step(i, _):
        at = pl.ds(pl.multiple_of(i * block, block), block)
        line = first_ref[at, :] + time_step * sum_ref[at, :].astype(f32)
        field_ref[at, :] = line
        rounded = line.astype(bf16)
        one_ref[at, :] = rounded[:, :half]
        two_ref[at, :] = rounded[:, half:]
        side_ref[at, :] = line[:, :side] if low else line[:, line.shape[1] - side:]
        return 0

    lax.fori_loop(0, first_ref.shape[0] // block, step, 0)


def meet(first, total, columns, low):
    modes, cells = first.shape
    vmem = pl.BlockSpec(memory_space=pltpu.VMEM)
    return pl.pallas_call(
        functools.partial(meet_kernel, low),
        in_specs=[vmem] * 2,
        out_specs=[vmem] * 4,
        out_shape=[
            jax.ShapeDtypeStruct((modes, cells), f32),
            jax.ShapeDtypeStruct((modes, cells // 2), bf16),
            jax.ShapeDtypeStruct((modes, cells // 2), bf16),
            jax.ShapeDtypeStruct((modes, 2 * columns), f32),
        ],
        name="meet",
        **small(12),
    )(first, total)


def cast_kernel(w_ref, out_ref):
    block = w_ref.shape[0]
    out_ref[pl.ds(pl.multiple_of(pl.program_id(0) * block, block), block), :] = w_ref[...].astype(bf16)


def cast(weights):
    block = 128
    return pl.pallas_call(
        cast_kernel,
        grid=(weights.shape[0] // block,),
        in_specs=[pl.BlockSpec((block, weights.shape[1]), lambda i: (i, 0))],
        out_specs=pl.BlockSpec(memory_space=pltpu.VMEM),
        out_shape=jax.ShapeDtypeStruct(weights.shape, bf16),
        name="cast",
        **small(36),
    )(weights)


def product(w_ref, span, parts, ours):
    plane = lax.axis_index("mode")
    beside = plane + 1 - 2 * lax.rem(plane, 2)
    owner = {0: plane, 1: beside, 2: 3 - plane, 3: 3 - beside}
    if not ours:
        skipped = jnp.where(plane < 2, 1, 0)
        owner = {j: jnp.clip(of - skipped, 0, 2) for j, of in owner.items()}
    total = None
    for j, pieces in parts.items():
        depth = pieces[0].shape[0]
        at = pl.multiple_of(owner[j] * depth, depth)
        weights = w_ref[span, pl.ds(at, depth)]
        terms = [jnp.dot(weights, piece[...], preferred_element_type=f32) for piece in pieces]
        term = terms[0] if len(terms) == 1 else jnp.concatenate(terms, axis=1)
        total = term if total is None else total + term
    return total


def parts_of(counts, refs):
    refs = iter(refs)
    return {j: [next(refs) for _ in range(count)] for j, count in counts.items()}


def own_kernel(counts, w_ref, *refs):
    *part_refs, base_ref, first_ref, rounded_ref = refs
    parts = parts_of(counts, part_refs)
    half = w_ref.shape[0] // 2
    for span in (slice(0, half), slice(half, 2 * half)):
        line = base_ref[span, :] + time_step * product(w_ref, span, parts, True)
        first_ref[span, :] = line
        rounded_ref[span, :] = line.astype(bf16)


def sum_kernel(counts, cut, this_ref, other_ref, *refs):
    *part_refs, sum_ref = refs
    parts = parts_of(counts, part_refs)
    if cut is not None:
        parts[2] = [parts[2][0].at[:, cut]]
    share = this_ref.shape[0] // 4
    x, y, core = place()
    for w_ref, of_core in ((this_ref, core), (other_ref, 1 - core)):
        total = product(w_ref, slice(None), parts, False).astype(bf16)
        for k, (of_x, of_y) in enumerate(((x, y), (1 - x, y), (x, 1 - y), (1 - x, 1 - y))):
            at = pl.multiple_of((4 * of_y + 2 * of_x + of_core) * share, share)
            sum_ref[pl.ds(at, share), :] = total[k * share:(k + 1) * share]


def place():
    tile = lax.axis_index("tile")
    return lax.rem(tile // 2, 2), tile // 4, lax.rem(tile, 2)


def gains(kernel, arrays, shape, kinds):
    vmem = pl.BlockSpec(memory_space=pltpu.VMEM)
    return pl.pallas_call(
        kernel,
        in_specs=[vmem] * len(arrays),
        out_specs=[vmem] * len(kinds),
        out_shape=[jax.ShapeDtypeStruct(shape, kind) for kind in kinds],
        name=kernel.func.__name__,
        **small(12),
    )(*arrays)


def own_rows(weights, x, a, b, c, based):
    parts = {0: x, 1: a, 2: b, 3: c}
    kernel = functools.partial(own_kernel, {j: len(part) for j, part in parts.items()})
    return gains(kernel, (weights, *x, *a, *b, *c, based), based.shape, (f32, bf16))


def end_sum(weights, x, b, c, cut=None):
    kernel = functools.partial(sum_kernel, {0: 1, 2: 1, 3: 1}, cut)
    return gains(kernel, (*weights, x, b, c), x.shape, (bf16,))[0]


def stack_kernel(*refs):
    out_ref = refs[-1]
    share = refs[0].shape[0]
    for k, ref in enumerate(refs[:-1]):
        out_ref[k * share:(k + 1) * share, :] = ref[...]


def stack(*pieces):
    share, depth = pieces[0].shape
    vmem = pl.BlockSpec(memory_space=pltpu.VMEM)
    return pl.pallas_call(
        stack_kernel,
        in_specs=[vmem] * len(pieces),
        out_specs=vmem,
        out_shape=jax.ShapeDtypeStruct((len(pieces) * share, depth), bf16),
        name="stack",
        **small(12),
    )(*pieces)


def unpack_kernel(rows, modes, *refs):
    *sum_refs, out_ref = refs[2:]
    columns = out_ref.shape[1]
    half, quarter = rows // 2, rows // 4
    for r in range(rows):
        at = slice(r % half * columns, (r % half + 1) * columns)
        of = slice(r % quarter * columns, (r % quarter + 1) * columns)
        line = refs[r // half][:, at] + time_step * sum_refs[r // quarter][:, of].astype(f32)
        out_ref[pl.ds(r, modes, stride=rows), :] = line


def unpack(firsts, sums, rows):
    modes, cells = firsts[0].shape
    columns = 2 * cells // rows
    block = 256
    spec = lambda count: pl.BlockSpec((block, count), lambda i: (i, 0))
    flat = pl.pallas_call(
        functools.partial(unpack_kernel, rows, block),
        grid=(modes // block,),
        in_specs=[spec(cells)] * 2 + [spec(cells // 2)] * 4,
        out_specs=pl.BlockSpec((block * rows, columns), lambda i: (i, 0)),
        out_shape=jax.ShapeDtypeStruct((modes * rows, columns), f32),
        name="unpack",
        **small(12),
    )(*firsts, *sums)
    return flat.reshape(modes, rows, columns)


inward = [(0, 1), (3, 2)]
outward = [(1, 0), (2, 3)]
across = [(1, 2), (2, 1)]


def line_of_four(distribution, courant, relax_rate, scatter_weight, cell_flags):
    modes, rows, columns = distribution.shape
    count = lax.axis_size("tile")
    up = [(i, i + 1) for i in range(count - 1)]
    down = [(i + 1, i) for i in range(count - 1)]
    send = functools.partial(lax.ppermute, axis_name="mode")
    after = lambda value, *earlier: lax.optimization_barrier((value, *earlier))[0]
    local = functools.partial(base, courant=courant, rate=relax_rate, flags=cell_flags)
    by = lambda value, bits: lax.ppermute(value, "tile", [(i, i ^ bits) for i in range(count)])

    piece = piece_of(scatter_weight, count)
    x1, x2, low, high = pack(distribution)
    piece = send(piece, perm=inward)
    b1 = send(x1, perm=across)
    b2 = send(after(x2, b1), perm=across)
    before = lax.ppermute(high, "tile", up)
    behind = lax.ppermute(low, "tile", down)
    a1 = send(x1, perm=inward)
    own_w = cast(after(scatter_weight, x1))
    base1, base2 = local([distribution], before, behind)
    from_piece = after(piece, own_w)
    px, py, pd = by(from_piece, 2), by(from_piece, 4), by(from_piece, 6)
    a2 = send(after(x2, a1, pd), perm=inward)
    c1 = send(after(a1, base1), perm=across)
    this = stack(after(piece, b2), px, py, pd)
    c2 = send(after(a2, this, pd), perm=across)
    edge_w = (this, by(after(this, a2, c1), 1))
    first1, own1 = own_rows(own_w, [x1], [a1], [b1], [c1], base1)
    sum1 = end_sum(edge_w, after(x1, own1), b1, c1)
    sum2 = end_sum(edge_w, x2, b2, c2)
    first2, own2 = own_rows(own_w, [after(x2, sum2)], [a2], [b2], [c2], base2)

    b1 = send(own1, perm=across)
    b2 = send(own2, perm=across)
    field1, x1, y1, low = meet(first1, send(sum1, perm=outward), columns, True)
    a1 = send(after(x1, b1), perm=inward)
    d1 = send(after(y1, b1), perm=inward)
    field2, x2, y2, high = meet(first2, send(sum2, perm=outward), columns, False)
    a2 = send(after(x2, b2), perm=inward)
    d2 = send(after(y2, b2, a2), perm=inward)
    c1 = send(a1, perm=across)
    e1 = send(d1, perm=across)
    half = b1.shape[1] // 2
    left, right = slice(0, half), slice(half, 2 * half)
    sum1 = end_sum(edge_w, x1, b1, c1, left)
    out1 = send(sum1, perm=outward)
    rum1 = end_sum(edge_w, y1, b1, e1, right)
    rut1 = send(after(rum1, out1), perm=outward)
    before = lax.ppermute(after(high, b2, d1), "tile", up)
    behind = lax.ppermute(after(low, b2, d1), "tile", down)
    base1, base2 = local([field1, field2], before, behind)
    c2 = send(a2, perm=across)
    e2 = send(after(d2, c2), perm=across)
    sum2 = end_sum(edge_w, after(x2, rum1, before), b2, c2, left)
    out2 = send(after(sum2, rut1, out1), perm=outward)
    rum2 = end_sum(edge_w, after(y2, sum2, base1), b2, e2, right)
    first1, _ = own_rows(own_w, [x1, y1], [a1, d1], [b1], [c1, e1], base1)
    rut2 = send(after(rum2, out2), perm=outward)
    first2, _ = own_rows(own_w, [after(x2, sum2), y2], [a2, d2], [b2], [c2, e2], base2)
    return unpack([first1, first2], [out1, rut1, out2, rut2], rows)


def extended(block, width):
    count = lax.axis_size("tile")
    up = [(i, i + 1) for i in range(count - 1)]
    down = [(i + 1, i) for i in range(count - 1)]
    low = lax.ppermute(block[:, -width:], "tile", up)
    high = lax.ppermute(block[:, :width], "tile", down)
    return jnp.concatenate([low, block, high], axis=1)


def gathered(distribution, courant, relax_rate, scatter_weight, cell_flags):
    cx = courant[0][:, None, None]
    cy = courant[1][:, None, None]
    rate = relax_rate[:, None, None]
    flags = cell_flags.astype(f32)[None]
    weight = scatter_weight.astype(bf16)
    field = distribution
    for step in range(2):
        full = jnp.pad(extended(field, 2), ((0, 0), (0, 0), (2, 2)))
        centre = full[:, 2:-2, 2:-2]
        back_x = 1.5 * centre - 2.0 * full[:, 1:-3, 2:-2] + 0.5 * full[:, :-4, 2:-2]
        fwd_x = -1.5 * centre + 2.0 * full[:, 3:-1, 2:-2] - 0.5 * full[:, 4:, 2:-2]
        back_y = 1.5 * centre - 2.0 * full[:, 2:-2, 1:-3] + 0.5 * full[:, 2:-2, :-4]
        fwd_y = -1.5 * centre + 2.0 * full[:, 2:-2, 3:-1] - 0.5 * full[:, 2:-2, 4:]
        transport = (
            jnp.maximum(cx, 0.0) * back_x
            + jnp.minimum(cx, 0.0) * fwd_x
            + jnp.maximum(cy, 0.0) * back_y
            + jnp.minimum(cy, 0.0) * fwd_y
        )
        flat = field.astype(bf16).reshape(field.shape[0], -1)
        flat = lax.all_gather(flat, "mode", axis=0, tiled=True)
        gain = jnp.dot(weight, flat, preferred_element_type=f32).reshape(field.shape)
        field = field - transport + time_step * (gain - rate * field - wall_rate * flags * field)
    return field


def body(*args):
    if lax.axis_size("mode") == 4 and lax.axis_size("tile") == 8 and args[0].shape[1] % 4 == 0:
        return line_of_four(*args)
    return gathered(*args)


def solution(mesh):
    in_specs = (
        P("mode", "tile", None),
        P(None, "mode"),
        P("mode"),
        P("mode", None),
        P("tile", None),
    )
    out_specs = P("mode", "tile", None)
    return jax.shard_map(body, mesh=mesh, in_specs=in_specs, out_specs=out_specs, check_vma=False)
```

```python
import functools

import jax
import jax.numpy as jnp
from jax import lax
from jax.experimental import pallas as pl
from jax.experimental.pallas import tpu as pltpu
from jax.sharding import PartitionSpec as P

time_step = 0.25
wall_rate = 2.0
bf16 = jnp.bfloat16
f32 = jnp.float32


def small(limit):
    return dict(
        cost_estimate=pl.CostEstimate(flops=1000, bytes_accessed=1000, transcendentals=0),
        compiler_params=pltpu.CompilerParams(vmem_limit_bytes=limit * 2**20),
    )


def pack_kernel(blocks, field_ref, one_ref, two_ref, low_ref, high_ref, held_ref, done_ref):
    modes, cells = one_ref.shape
    columns = field_ref.shape[1]
    half = cells // columns
    rows = 2 * half
    block = modes // blocks
    copies = []
    for i in range(blocks):
        at = pl.ds(i * block * rows, block * rows)
        copies.append(pltpu.make_async_copy(field_ref.at[at], held_ref.at[at], done_ref.at[i]))
        copies[i].start()
    for i in range(blocks):
        copies[i].wait()
        to = slice(i * block, (i + 1) * block)
        for r in range(rows):
            line = held_ref[pl.ds(i * block * rows + r, block, stride=rows), :]
            to_ref = one_ref if r < half else two_ref
            to_ref[to, r % half * columns:(r % half + 1) * columns] = line.astype(bf16)
            if r < 2:
                low_ref[to, r * columns:(r + 1) * columns] = line
            if r >= rows - 2:
                at = r - rows + 2
                high_ref[to, at * columns:(at + 1) * columns] = line


def pack(field):
    modes, rows, columns = field.shape
    blocks = 4
    shape = lambda count, kind: jax.ShapeDtypeStruct((modes, count * columns), kind)
    return pl.pallas_call(
        functools.partial(pack_kernel, blocks),
        in_specs=[pl.BlockSpec(memory_space=pl.ANY)],
        out_specs=[pl.BlockSpec(memory_space=pltpu.VMEM)] * 4,
        out_shape=[shape(rows // 2, bf16)] * 2 + [shape(2, f32)] * 2,
        scratch_shapes=[pltpu.VMEM((modes * rows, columns), f32), pltpu.SemaphoreType.DMA((blocks,))],
        name="pack",
        **small(46),
    )(field.reshape(modes * rows, columns))


def local_line(lines, r, params, flags):
    cx, cy, rate = params
    centre = lines(r)
    lane = lax.broadcasted_iota(jnp.int32, centre.shape, 1)
    columns = centre.shape[1]

    def moved(by):
        turned = pltpu.roll(centre, by % columns, 1)
        keep = lane >= by if by > 0 else lane < columns + by
        return jnp.where(keep, turned, 0.0)

    back_x = 1.5 * centre - 2.0 * lines(r - 1) + 0.5 * lines(r - 2)
    fwd_x = -1.5 * centre + 2.0 * lines(r + 1) - 0.5 * lines(r + 2)
    back_y = 1.5 * centre - 2.0 * moved(1) + 0.5 * moved(2)
    fwd_y = -1.5 * centre + 2.0 * moved(-1) - 0.5 * moved(-2)
    transport = (
        jnp.maximum(cx, 0.0) * back_x
        + jnp.minimum(cx, 0.0) * fwd_x
        + jnp.maximum(cy, 0.0) * back_y
        + jnp.minimum(cy, 0.0) * fwd_y
    )
    return centre - transport - time_step * (rate * centre + wall_rate * flags * centre)


def column(line):
    count = line.shape[1]
    at = lax.broadcasted_iota(jnp.int32, (count, count), 0)
    lane = lax.broadcasted_iota(jnp.int32, (count, count), 1)
    return jnp.sum(jnp.where(at == lane, line, 0.0), axis=1, keepdims=True)


def base_kernel(rows, modes, strided, *refs):
    *field_refs, before_ref, behind_ref, courant_ref, rate_ref, flags_ref, one_ref, two_ref = refs
    params = (column(courant_ref[0:1, :]), column(courant_ref[1:2, :]), column(rate_ref[...]))
    flags = flags_ref[...].astype(f32)
    columns = flags_ref.shape[1]
    half = rows // 2
    cut = lambda at: slice(at * columns, (at + 1) * columns)

    def lines(r):
        if r < 0:
            return before_ref[:, cut(r + 2)]
        if r >= rows:
            return behind_ref[:, cut(r - rows)]
        if strided:
            return field_refs[0][pl.ds(r, modes, stride=rows), :]
        return field_refs[r // half][:, cut(r % half)]

    for r in range(rows):
        to_ref = one_ref if r < half else two_ref
        to_ref[:, cut(r % half)] = local_line(lines, r, params, flags[r:r + 1, :])


def base(fields, before, behind, courant, rate, flags):
    rows, columns = flags.shape
    modes = before.shape[0]
    block = 128
    spec = lambda count: pl.BlockSpec((block, count * columns), lambda i: (i, 0))
    strided = len(fields) == 1
    if strided:
        field_specs = [pl.BlockSpec((block * rows, columns), lambda i: (i, 0))]
        fields = [fields[0].reshape(modes * rows, columns)]
    else:
        field_specs = [spec(rows // 2)] * 2
    per_mode = lambda count: pl.BlockSpec((count, block), lambda i: (0, i))
    return pl.pallas_call(
        functools.partial(base_kernel, rows, block, strided),
        grid=(modes // block,),
        in_specs=field_specs + [spec(2), spec(2), per_mode(2), per_mode(1), pl.BlockSpec((rows, columns), lambda i: (0, 0))],
        out_specs=[spec(rows // 2)] * 2,
        out_shape=[jax.ShapeDtypeStruct((modes, rows // 2 * columns), f32)] * 2,
        name="base",
        **small(12),
    )(*fields, before, behind, courant, rate.reshape(1, modes), flags)


def piece_kernel(w_ref, out_ref, held_ref, done_ref):
    share, kept = out_ref.shape
    at = pl.multiple_of(lax.axis_index("tile") * share, share)
    skipped = w_ref.shape[1] - kept
    left = pl.multiple_of(jnp.where(lax.axis_index("mode") == 0, skipped, 0), skipped)
    copy = pltpu.make_async_copy(w_ref.at[pl.ds(at, share), pl.ds(left, kept)], held_ref, done_ref)
    copy.start()
    copy.wait()
    out_ref[...] = held_ref[...].astype(bf16)


def piece_of(weights, count):
    modes, depth = weights.shape
    shape = (modes // count, depth - modes)
    return pl.pallas_call(
        piece_kernel,
        in_specs=[pl.BlockSpec(memory_space=pl.ANY)],
        out_specs=pl.BlockSpec(memory_space=pltpu.VMEM),
        out_shape=jax.ShapeDtypeStruct(shape, bf16),
        scratch_shapes=[pltpu.VMEM(shape, f32), pltpu.SemaphoreType.DMA],
        name="piece",
        **small(56),
    )(weights)


def meet_kernel(low, first_ref, sum_ref, field_ref, one_ref, two_ref, side_ref):
    block = 128
    half = one_ref.shape[1]
    side = side_ref.shape[1]

    def step(i, _):
        at = pl.ds(pl.multiple_of(i * block, block), block)
        line = first_ref[at, :] + time_step * sum_ref[at, :].astype(f32)
        field_ref[at, :] = line
        rounded = line.astype(bf16)
        one_ref[at, :] = rounded[:, :half]
        two_ref[at, :] = rounded[:, half:]
        side_ref[at, :] = line[:, :side] if low else line[:, line.shape[1] - side:]
        return 0

    lax.fori_loop(0, first_ref.shape[0] // block, step, 0)


def meet(first, total, columns, low):
    modes, cells = first.shape
    vmem = pl.BlockSpec(memory_space=pltpu.VMEM)
    return pl.pallas_call(
        functools.partial(meet_kernel, low),
        in_specs=[vmem] * 2,
        out_specs=[vmem] * 4,
        out_shape=[
            jax.ShapeDtypeStruct((modes, cells), f32),
            jax.ShapeDtypeStruct((modes, cells // 2), bf16),
            jax.ShapeDtypeStruct((modes, cells // 2), bf16),
            jax.ShapeDtypeStruct((modes, 2 * columns), f32),
        ],
        name="meet",
        **small(12),
    )(first, total)


def cast_kernel(w_ref, out_ref):
    block = w_ref.shape[0]
    out_ref[pl.ds(pl.multiple_of(pl.program_id(0) * block, block), block), :] = w_ref[...].astype(bf16)


def cast(weights):
    block = 128
    return pl.pallas_call(
        cast_kernel,
        grid=(weights.shape[0] // block,),
        in_specs=[pl.BlockSpec((block, weights.shape[1]), lambda i: (i, 0))],
        out_specs=pl.BlockSpec(memory_space=pltpu.VMEM),
        out_shape=jax.ShapeDtypeStruct(weights.shape, bf16),
        name="cast",
        **small(36),
    )(weights)


def product(w_ref, span, parts, ours):
    plane = lax.axis_index("mode")
    beside = plane + 1 - 2 * lax.rem(plane, 2)
    owner = {0: plane, 1: beside, 2: 3 - plane, 3: 3 - beside}
    if not ours:
        skipped = jnp.where(plane < 2, 1, 0)
        owner = {j: jnp.clip(of - skipped, 0, 2) for j, of in owner.items()}
    total = None
    for j, pieces in parts.items():
        depth = pieces[0].shape[0]
        at = pl.multiple_of(owner[j] * depth, depth)
        weights = w_ref[span, pl.ds(at, depth)]
        terms = [jnp.dot(weights, piece[...], preferred_element_type=f32) for piece in pieces]
        term = terms[0] if len(terms) == 1 else jnp.concatenate(terms, axis=1)
        total = term if total is None else total + term
    return total


def parts_of(counts, refs):
    refs = iter(refs)
    return {j: [next(refs) for _ in range(count)] for j, count in counts.items()}


def own_kernel(counts, w_ref, *refs):
    *part_refs, base_ref, first_ref, rounded_ref = refs
    parts = parts_of(counts, part_refs)
    half = w_ref.shape[0] // 2
    for span in (slice(0, half), slice(half, 2 * half)):
        line = base_ref[span, :] + time_step * product(w_ref, span, parts, True)
        first_ref[span, :] = line
        rounded_ref[span, :] = line.astype(bf16)


def sum_kernel(counts, cut, this_ref, other_ref, *refs):
    *part_refs, sum_ref = refs
    parts = parts_of(counts, part_refs)
    if cut is not None:
        parts[2] = [parts[2][0].at[:, cut]]
    share = this_ref.shape[0] // 4
    x, y, core = place()
    for w_ref, of_core in ((this_ref, core), (other_ref, 1 - core)):
        total = product(w_ref, slice(None), parts, False).astype(bf16)
        for k, (of_x, of_y) in enumerate(((x, y), (1 - x, y), (x, 1 - y), (1 - x, 1 - y))):
            at = pl.multiple_of((4 * of_y + 2 * of_x + of_core) * share, share)
            sum_ref[pl.ds(at, share), :] = total[k * share:(k + 1) * share]


def place():
    tile = lax.axis_index("tile")
    return lax.rem(tile // 2, 2), tile // 4, lax.rem(tile, 2)


def gains(kernel, arrays, shape, kinds):
    vmem = pl.BlockSpec(memory_space=pltpu.VMEM)
    return pl.pallas_call(
        kernel,
        in_specs=[vmem] * len(arrays),
        out_specs=[vmem] * len(kinds),
        out_shape=[jax.ShapeDtypeStruct(shape, kind) for kind in kinds],
        name=kernel.func.__name__,
        **small(12),
    )(*arrays)


def own_rows(weights, x, a, b, c, based):
    parts = {0: x, 1: a, 2: b, 3: c}
    kernel = functools.partial(own_kernel, {j: len(part) for j, part in parts.items()})
    return gains(kernel, (weights, *x, *a, *b, *c, based), based.shape, (f32, bf16))


def end_sum(weights, x, b, c, cut=None):
    kernel = functools.partial(sum_kernel, {0: 1, 2: 1, 3: 1}, cut)
    return gains(kernel, (*weights, x, b, c), x.shape, (bf16,))[0]


def stack_kernel(*refs):
    out_ref = refs[-1]
    share = refs[0].shape[0]
    for k, ref in enumerate(refs[:-1]):
        out_ref[k * share:(k + 1) * share, :] = ref[...]


def stack(*pieces):
    share, depth = pieces[0].shape
    vmem = pl.BlockSpec(memory_space=pltpu.VMEM)
    return pl.pallas_call(
        stack_kernel,
        in_specs=[vmem] * len(pieces),
        out_specs=vmem,
        out_shape=jax.ShapeDtypeStruct((len(pieces) * share, depth), bf16),
        name="stack",
        **small(12),
    )(*pieces)


def unpack_kernel(rows, modes, *refs):
    *sum_refs, out_ref = refs[2:]
    columns = out_ref.shape[1]
    half, quarter = rows // 2, rows // 4
    for r in range(rows):
        at = slice(r % half * columns, (r % half + 1) * columns)
        of = slice(r % quarter * columns, (r % quarter + 1) * columns)
        line = refs[r // half][:, at] + time_step * sum_refs[r // quarter][:, of].astype(f32)
        out_ref[pl.ds(r, modes, stride=rows), :] = line


def unpack(firsts, sums, rows):
    modes, cells = firsts[0].shape
    columns = 2 * cells // rows
    block = 256
    spec = lambda count: pl.BlockSpec((block, count), lambda i: (i, 0))
    flat = pl.pallas_call(
        functools.partial(unpack_kernel, rows, block),
        grid=(modes // block,),
        in_specs=[spec(cells)] * 2 + [spec(cells // 2)] * 4,
        out_specs=pl.BlockSpec((block * rows, columns), lambda i: (i, 0)),
        out_shape=jax.ShapeDtypeStruct((modes * rows, columns), f32),
        name="unpack",
        **small(12),
    )(*firsts, *sums)
    return flat.reshape(modes, rows, columns)


inward = [(0, 1), (3, 2)]
outward = [(1, 0), (2, 3)]
across = [(1, 2), (2, 1)]


def line_of_four(distribution, courant, relax_rate, scatter_weight, cell_flags):
    modes, rows, columns = distribution.shape
    count = lax.axis_size("tile")
    up = [(i, i + 1) for i in range(count - 1)]
    down = [(i + 1, i) for i in range(count - 1)]
    send = functools.partial(lax.ppermute, axis_name="mode")
    after = lambda value, *earlier: lax.optimization_barrier((value, *earlier))[0]
    local = functools.partial(base, courant=courant, rate=relax_rate, flags=cell_flags)
    by = lambda value, bits: lax.ppermute(value, "tile", [(i, i ^ bits) for i in range(count)])

    piece = piece_of(scatter_weight, count)
    x1, x2, low, high = pack(distribution)
    piece = send(piece, perm=inward)
    b1 = send(x1, perm=across)
    b2 = send(after(x2, b1), perm=across)
    before = lax.ppermute(high, "tile", up)
    behind = lax.ppermute(low, "tile", down)
    a1 = send(x1, perm=inward)
    own_w = cast(after(scatter_weight, x1))
    base1, base2 = local([distribution], before, behind)
    from_piece = after(piece, own_w)
    px, py, pd = by(from_piece, 2), by(from_piece, 4), by(from_piece, 6)
    a2 = send(after(x2, a1, pd), perm=inward)
    c1 = send(after(a1, base1), perm=across)
    this = stack(after(piece, b2), px, py, pd)
    c2 = send(after(a2, this, pd), perm=across)
    edge_w = (this, by(after(this, a2, c1), 1))
    first1, own1 = own_rows(own_w, [x1], [a1], [b1], [c1], base1)
    sum1 = end_sum(edge_w, after(x1, own1), b1, c1)
    sum2 = end_sum(edge_w, x2, b2, c2)
    first2, own2 = own_rows(own_w, [after(x2, sum2)], [a2], [b2], [c2], base2)

    b1 = send(own1, perm=across)
    b2 = send(own2, perm=across)
    field1, x1, y1, low = meet(first1, send(sum1, perm=outward), columns, True)
    a1 = send(x1, perm=inward)
    d1 = send(after(y1, b1), perm=inward)
    field2, x2, y2, high = meet(first2, send(sum2, perm=outward), columns, False)
    a2 = send(x2, perm=inward)
    d2 = send(after(y2, a2), perm=inward)
    c1 = send(a1, perm=across)
    e1 = send(d1, perm=across)
    half = b1.shape[1] // 2
    left, right = slice(0, half), slice(half, 2 * half)
    sum1 = end_sum(edge_w, x1, b1, c1, left)
    out1 = send(sum1, perm=outward)
    rum1 = end_sum(edge_w, y1, b1, e1, right)
    rut1 = send(after(rum1, out1), perm=outward)
    before = lax.ppermute(after(high, b2, d1), "tile", up)
    behind = lax.ppermute(after(low, b2, d1), "tile", down)
    base1, base2 = local([field1, field2], before, behind)
    c2 = send(a2, perm=across)
    e2 = send(after(d2, c2), perm=across)
    sum2 = end_sum(edge_w, after(x2, rum1, before), b2, c2, left)
    out2 = send(after(sum2, rut1, out1), perm=outward)
    rum2 = end_sum(edge_w, after(y2, sum2, base1), b2, e2, right)
    first1, _ = own_rows(own_w, [x1, y1], [a1, d1], [b1], [c1, e1], base1)
    rut2 = send(after(rum2, out2), perm=outward)
    first2, _ = own_rows(own_w, [after(x2, sum2), y2], [a2, d2], [b2], [c2, e2], base2)
    return unpack([first1, first2], [out1, rut1, out2, rut2], rows)


def extended(block, width):
    count = lax.axis_size("tile")
    up = [(i, i + 1) for i in range(count - 1)]
    down = [(i + 1, i) for i in range(count - 1)]
    low = lax.ppermute(block[:, -width:], "tile", up)
    high = lax.ppermute(block[:, :width], "tile", down)
    return jnp.concatenate([low, block, high], axis=1)


def gathered(distribution, courant, relax_rate, scatter_weight, cell_flags):
    cx = courant[0][:, None, None]
    cy = courant[1][:, None, None]
    rate = relax_rate[:, None, None]
    flags = cell_flags.astype(f32)[None]
    weight = scatter_weight.astype(bf16)
    field = distribution
    for step in range(2):
        full = jnp.pad(extended(field, 2), ((0, 0), (0, 0), (2, 2)))
        centre = full[:, 2:-2, 2:-2]
        back_x = 1.5 * centre - 2.0 * full[:, 1:-3, 2:-2] + 0.5 * full[:, :-4, 2:-2]
        fwd_x = -1.5 * centre + 2.0 * full[:, 3:-1, 2:-2] - 0.5 * full[:, 4:, 2:-2]
        back_y = 1.5 * centre - 2.0 * full[:, 2:-2, 1:-3] + 0.5 * full[:, 2:-2, :-4]
        fwd_y = -1.5 * centre + 2.0 * full[:, 2:-2, 3:-1] - 0.5 * full[:, 2:-2, 4:]
        transport = (
            jnp.maximum(cx, 0.0) * back_x
            + jnp.minimum(cx, 0.0) * fwd_x
            + jnp.maximum(cy, 0.0) * back_y
            + jnp.minimum(cy, 0.0) * fwd_y
        )
        flat = field.astype(bf16).reshape(field.shape[0], -1)
        flat = lax.all_gather(flat, "mode", axis=0, tiled=True)
        gain = jnp.dot(weight, flat, preferred_element_type=f32).reshape(field.shape)
        field = field - transport + time_step * (gain - rate * field - wall_rate * flags * field)
    return field


def body(*args):
    if lax.axis_size("mode") == 4 and lax.axis_size("tile") == 8 and args[0].shape[1] % 4 == 0:
        return line_of_four(*args)
    return gathered(*args)


def solution(mesh):
    in_specs = (
        P("mode", "tile", None),
        P(None, "mode"),
        P("mode"),
        P("mode", None),
        P("tile", None),
    )
    out_specs = P("mode", "tile", None)
    return jax.shard_map(body, mesh=mesh, in_specs=in_specs, out_specs=out_specs, check_vma=False)
```

```python
import functools

import jax
import jax.numpy as jnp
from jax import lax
from jax.experimental import pallas as pl
from jax.experimental.pallas import tpu as pltpu
from jax.sharding import PartitionSpec as P

time_step = 0.25
wall_rate = 2.0
bf16 = jnp.bfloat16
f32 = jnp.float32


def small(limit):
    return dict(
        cost_estimate=pl.CostEstimate(flops=1000, bytes_accessed=1000, transcendentals=0),
        compiler_params=pltpu.CompilerParams(vmem_limit_bytes=limit * 2**20),
    )


def pack_kernel(blocks, field_ref, one_ref, two_ref, low_ref, high_ref, held_ref, done_ref):
    modes, cells = one_ref.shape
    columns = field_ref.shape[1]
    half = cells // columns
    rows = 2 * half
    block = modes // blocks
    copies = []
    for i in range(blocks):
        at = pl.ds(i * block * rows, block * rows)
        copies.append(pltpu.make_async_copy(field_ref.at[at], held_ref.at[at], done_ref.at[i]))
        copies[i].start()
    for i in range(blocks):
        copies[i].wait()
        to = slice(i * block, (i + 1) * block)
        for r in range(rows):
            line = held_ref[pl.ds(i * block * rows + r, block, stride=rows), :]
            to_ref = one_ref if r < half else two_ref
            to_ref[to, r % half * columns:(r % half + 1) * columns] = line.astype(bf16)
            if r < 2:
                low_ref[to, r * columns:(r + 1) * columns] = line
            if r >= rows - 2:
                at = r - rows + 2
                high_ref[to, at * columns:(at + 1) * columns] = line


def pack(field):
    modes, rows, columns = field.shape
    blocks = 4
    shape = lambda count, kind: jax.ShapeDtypeStruct((modes, count * columns), kind)
    return pl.pallas_call(
        functools.partial(pack_kernel, blocks),
        in_specs=[pl.BlockSpec(memory_space=pl.ANY)],
        out_specs=[pl.BlockSpec(memory_space=pltpu.VMEM)] * 4,
        out_shape=[shape(rows // 2, bf16)] * 2 + [shape(2, f32)] * 2,
        scratch_shapes=[pltpu.VMEM((modes * rows, columns), f32), pltpu.SemaphoreType.DMA((blocks,))],
        name="pack",
        **small(46),
    )(field.reshape(modes * rows, columns))


def local_line(lines, r, params, flags):
    cx, cy, rate = params
    centre = lines(r)
    lane = lax.broadcasted_iota(jnp.int32, centre.shape, 1)
    columns = centre.shape[1]

    def moved(by):
        turned = pltpu.roll(centre, by % columns, 1)
        keep = lane >= by if by > 0 else lane < columns + by
        return jnp.where(keep, turned, 0.0)

    back_x = 1.5 * centre - 2.0 * lines(r - 1) + 0.5 * lines(r - 2)
    fwd_x = -1.5 * centre + 2.0 * lines(r + 1) - 0.5 * lines(r + 2)
    back_y = 1.5 * centre - 2.0 * moved(1) + 0.5 * moved(2)
    fwd_y = -1.5 * centre + 2.0 * moved(-1) - 0.5 * moved(-2)
    transport = (
        jnp.maximum(cx, 0.0) * back_x
        + jnp.minimum(cx, 0.0) * fwd_x
        + jnp.maximum(cy, 0.0) * back_y
        + jnp.minimum(cy, 0.0) * fwd_y
    )
    return centre - transport - time_step * (rate * centre + wall_rate * flags * centre)


def column(line):
    count = line.shape[1]
    at = lax.broadcasted_iota(jnp.int32, (count, count), 0)
    lane = lax.broadcasted_iota(jnp.int32, (count, count), 1)
    return jnp.sum(jnp.where(at == lane, line, 0.0), axis=1, keepdims=True)


def base_kernel(rows, modes, strided, *refs):
    *field_refs, before_ref, behind_ref, courant_ref, rate_ref, flags_ref, one_ref, two_ref = refs
    params = (column(courant_ref[0:1, :]), column(courant_ref[1:2, :]), column(rate_ref[...]))
    flags = flags_ref[...].astype(f32)
    columns = flags_ref.shape[1]
    half = rows // 2
    cut = lambda at: slice(at * columns, (at + 1) * columns)

    def lines(r):
        if r < 0:
            return before_ref[:, cut(r + 2)]
        if r >= rows:
            return behind_ref[:, cut(r - rows)]
        if strided:
            return field_refs[0][pl.ds(r, modes, stride=rows), :]
        return field_refs[r // half][:, cut(r % half)]

    for r in range(rows):
        to_ref = one_ref if r < half else two_ref
        to_ref[:, cut(r % half)] = local_line(lines, r, params, flags[r:r + 1, :])


def base(fields, before, behind, courant, rate, flags):
    rows, columns = flags.shape
    modes = before.shape[0]
    block = 128
    spec = lambda count: pl.BlockSpec((block, count * columns), lambda i: (i, 0))
    strided = len(fields) == 1
    if strided:
        field_specs = [pl.BlockSpec((block * rows, columns), lambda i: (i, 0))]
        fields = [fields[0].reshape(modes * rows, columns)]
    else:
        field_specs = [spec(rows // 2)] * 2
    per_mode = lambda count: pl.BlockSpec((count, block), lambda i: (0, i))
    return pl.pallas_call(
        functools.partial(base_kernel, rows, block, strided),
        grid=(modes // block,),
        in_specs=field_specs + [spec(2), spec(2), per_mode(2), per_mode(1), pl.BlockSpec((rows, columns), lambda i: (0, 0))],
        out_specs=[spec(rows // 2)] * 2,
        out_shape=[jax.ShapeDtypeStruct((modes, rows // 2 * columns), f32)] * 2,
        name="base",
        **small(12),
    )(*fields, before, behind, courant, rate.reshape(1, modes), flags)


def piece_kernel(w_ref, out_ref, held_ref, done_ref):
    share, kept = out_ref.shape
    at = pl.multiple_of(lax.axis_index("tile") * share, share)
    skipped = w_ref.shape[1] - kept
    left = pl.multiple_of(jnp.where(lax.axis_index("mode") == 0, skipped, 0), skipped)
    copy = pltpu.make_async_copy(w_ref.at[pl.ds(at, share), pl.ds(left, kept)], held_ref, done_ref)
    copy.start()
    copy.wait()
    out_ref[...] = held_ref[...].astype(bf16)


def piece_of(weights, count):
    modes, depth = weights.shape
    shape = (modes // count, depth - modes)
    return pl.pallas_call(
        piece_kernel,
        in_specs=[pl.BlockSpec(memory_space=pl.ANY)],
        out_specs=pl.BlockSpec(memory_space=pltpu.VMEM),
        out_shape=jax.ShapeDtypeStruct(shape, bf16),
        scratch_shapes=[pltpu.VMEM(shape, f32), pltpu.SemaphoreType.DMA],
        name="piece",
        **small(56),
    )(weights)


def meet_kernel(low, first_ref, sum_ref, field_ref, one_ref, two_ref, side_ref):
    block = 128
    half = one_ref.shape[1]
    side = side_ref.shape[1]

    def step(i, _):
        at = pl.ds(pl.multiple_of(i * block, block), block)
        line = first_ref[at, :] + time_step * sum_ref[at, :].astype(f32)
        field_ref[at, :] = line
        rounded = line.astype(bf16)
        one_ref[at, :] = rounded[:, :half]
        two_ref[at, :] = rounded[:, half:]
        side_ref[at, :] = line[:, :side] if low else line[:, line.shape[1] - side:]
        return 0

    lax.fori_loop(0, first_ref.shape[0] // block, step, 0)


def meet(first, total, columns, low):
    modes, cells = first.shape
    vmem = pl.BlockSpec(memory_space=pltpu.VMEM)
    return pl.pallas_call(
        functools.partial(meet_kernel, low),
        in_specs=[vmem] * 2,
        out_specs=[vmem] * 4,
        out_shape=[
            jax.ShapeDtypeStruct((modes, cells), f32),
            jax.ShapeDtypeStruct((modes, cells // 2), bf16),
            jax.ShapeDtypeStruct((modes, cells // 2), bf16),
            jax.ShapeDtypeStruct((modes, 2 * columns), f32),
        ],
        name="meet",
        **small(12),
    )(first, total)


def cast_kernel(w_ref, out_ref):
    block = w_ref.shape[0]
    out_ref[pl.ds(pl.multiple_of(pl.program_id(0) * block, block), block), :] = w_ref[...].astype(bf16)


def cast(weights):
    block = 128
    return pl.pallas_call(
        cast_kernel,
        grid=(weights.shape[0] // block,),
        in_specs=[pl.BlockSpec((block, weights.shape[1]), lambda i: (i, 0))],
        out_specs=pl.BlockSpec(memory_space=pltpu.VMEM),
        out_shape=jax.ShapeDtypeStruct(weights.shape, bf16),
        name="cast",
        **small(36),
    )(weights)


def product(w_ref, span, parts, ours):
    plane = lax.axis_index("mode")
    beside = plane + 1 - 2 * lax.rem(plane, 2)
    owner = {0: plane, 1: beside, 2: 3 - plane, 3: 3 - beside}
    if not ours:
        skipped = jnp.where(plane < 2, 1, 0)
        owner = {j: jnp.clip(of - skipped, 0, 2) for j, of in owner.items()}
    total = None
    for j, pieces in parts.items():
        depth = pieces[0].shape[0]
        at = pl.multiple_of(owner[j] * depth, depth)
        weights = w_ref[span, pl.ds(at, depth)]
        terms = [jnp.dot(weights, piece[...], preferred_element_type=f32) for piece in pieces]
        term = terms[0] if len(terms) == 1 else jnp.concatenate(terms, axis=1)
        total = term if total is None else total + term
    return total


def parts_of(counts, refs):
    refs = iter(refs)
    return {j: [next(refs) for _ in range(count)] for j, count in counts.items()}


def own_kernel(counts, w_ref, *refs):
    *part_refs, base_ref, first_ref, rounded_ref = refs
    parts = parts_of(counts, part_refs)
    half = w_ref.shape[0] // 2
    for span in (slice(0, half), slice(half, 2 * half)):
        line = base_ref[span, :] + time_step * product(w_ref, span, parts, True)
        first_ref[span, :] = line
        rounded_ref[span, :] = line.astype(bf16)


def early_kernel(counts, w_ref, *refs):
    *part_refs, out_ref = refs
    out_ref[...] = time_step * product(w_ref, slice(None), parts_of(counts, part_refs), True)


def late_kernel(counts, w_ref, *refs):
    *part_refs, base_ref, early_ref, out_ref = refs
    total = product(w_ref, slice(None), parts_of(counts, part_refs), True)
    out_ref[...] = base_ref[...] + early_ref[...] + time_step * total


def sum_kernel(counts, cut, this_ref, other_ref, *refs):
    *part_refs, sum_ref = refs
    parts = parts_of(counts, part_refs)
    if cut is not None:
        parts[2] = [parts[2][0].at[:, cut]]
    share = this_ref.shape[0] // 4
    x, y, core = place()
    for w_ref, of_core in ((this_ref, core), (other_ref, 1 - core)):
        total = product(w_ref, slice(None), parts, False).astype(bf16)
        for k, (of_x, of_y) in enumerate(((x, y), (1 - x, y), (x, 1 - y), (1 - x, 1 - y))):
            at = pl.multiple_of((4 * of_y + 2 * of_x + of_core) * share, share)
            sum_ref[pl.ds(at, share), :] = total[k * share:(k + 1) * share]


def place():
    tile = lax.axis_index("tile")
    return lax.rem(tile // 2, 2), tile // 4, lax.rem(tile, 2)


def gains(kernel, arrays, shape, kinds):
    vmem = pl.BlockSpec(memory_space=pltpu.VMEM)
    return pl.pallas_call(
        kernel,
        in_specs=[vmem] * len(arrays),
        out_specs=[vmem] * len(kinds),
        out_shape=[jax.ShapeDtypeStruct(shape, kind) for kind in kinds],
        name=kernel.func.__name__,
        **small(12),
    )(*arrays)


def own_rows(weights, x, a, b, c, based):
    parts = {0: x, 1: a, 2: b, 3: c}
    kernel = functools.partial(own_kernel, {j: len(part) for j, part in parts.items()})
    return gains(kernel, (weights, *x, *a, *b, *c, based), based.shape, (f32, bf16))


def early_rows(weights, x, b):
    kernel = functools.partial(early_kernel, {0: len(x), 2: 1})
    return gains(kernel, (weights, *x, b), b.shape, (f32,))[0]


def late_rows(weights, a, c, based, early):
    kernel = functools.partial(late_kernel, {1: len(a), 3: len(c)})
    return gains(kernel, (weights, *a, *c, based, early), based.shape, (f32,))[0]


def end_sum(weights, x, b, c, cut=None):
    kernel = functools.partial(sum_kernel, {0: 1, 2: 1, 3: 1}, cut)
    return gains(kernel, (*weights, x, b, c), x.shape, (bf16,))[0]


def stack_kernel(*refs):
    out_ref = refs[-1]
    share = refs[0].shape[0]
    for k, ref in enumerate(refs[:-1]):
        out_ref[k * share:(k + 1) * share, :] = ref[...]


def stack(*pieces):
    share, depth = pieces[0].shape
    vmem = pl.BlockSpec(memory_space=pltpu.VMEM)
    return pl.pallas_call(
        stack_kernel,
        in_specs=[vmem] * len(pieces),
        out_specs=vmem,
        out_shape=jax.ShapeDtypeStruct((len(pieces) * share, depth), bf16),
        name="stack",
        **small(12),
    )(*pieces)


def unpack_kernel(rows, modes, *refs):
    *sum_refs, out_ref = refs[2:]
    columns = out_ref.shape[1]
    half, quarter = rows // 2, rows // 4
    for r in range(rows):
        at = slice(r % half * columns, (r % half + 1) * columns)
        of = slice(r % quarter * columns, (r % quarter + 1) * columns)
        line = refs[r // half][:, at] + time_step * sum_refs[r // quarter][:, of].astype(f32)
        out_ref[pl.ds(r, modes, stride=rows), :] = line


def unpack(firsts, sums, rows):
    modes, cells = firsts[0].shape
    columns = 2 * cells // rows
    block = 128
    spec = lambda count: pl.BlockSpec((block, count), lambda i: (i, 0))
    flat = pl.pallas_call(
        functools.partial(unpack_kernel, rows, block),
        grid=(modes // block,),
        in_specs=[spec(cells)] * 2 + [spec(cells // 2)] * 4,
        out_specs=pl.BlockSpec((block * rows, columns), lambda i: (i, 0)),
        out_shape=jax.ShapeDtypeStruct((modes * rows, columns), f32),
        name="unpack",
        **small(12),
    )(*firsts, *sums)
    return flat.reshape(modes, rows, columns)


inward = [(0, 1), (3, 2)]
outward = [(1, 0), (2, 3)]
across = [(1, 2), (2, 1)]


def line_of_four(distribution, courant, relax_rate, scatter_weight, cell_flags):
    modes, rows, columns = distribution.shape
    count = lax.axis_size("tile")
    up = [(i, i + 1) for i in range(count - 1)]
    down = [(i + 1, i) for i in range(count - 1)]
    send = functools.partial(lax.ppermute, axis_name="mode")
    after = lambda value, *earlier: lax.optimization_barrier((value, *earlier))[0]
    local = functools.partial(base, courant=courant, rate=relax_rate, flags=cell_flags)
    by = lambda value, bits: lax.ppermute(value, "tile", [(i, i ^ bits) for i in range(count)])

    piece = piece_of(scatter_weight, count)
    x1, x2, low, high = pack(distribution)
    piece = send(piece, perm=inward)
    b1 = send(x1, perm=across)
    b2 = send(after(x2, b1), perm=across)
    before = lax.ppermute(high, "tile", up)
    behind = lax.ppermute(low, "tile", down)
    a1 = send(x1, perm=inward)
    own_w = cast(after(scatter_weight, x1))
    base1, base2 = local([distribution], before, behind)
    from_piece = after(piece, own_w)
    px, py, pd = by(from_piece, 2), by(from_piece, 4), by(from_piece, 6)
    a2 = send(after(x2, a1, pd), perm=inward)
    c1 = send(after(a1, base1), perm=across)
    this = stack(after(piece, b2), px, py, pd)
    c2 = send(after(a2, this, pd), perm=across)
    edge_w = (this, by(after(this, a2, c1), 1))
    first1, own1 = own_rows(own_w, [x1], [a1], [b1], [c1], base1)
    sum1 = end_sum(edge_w, after(x1, own1), b1, c1)
    sum2 = end_sum(edge_w, x2, b2, c2)
    first2, own2 = own_rows(own_w, [after(x2, sum2)], [a2], [b2], [c2], base2)

    b1 = send(own1, perm=across)
    b2 = send(own2, perm=across)
    field1, x1, y1, low = meet(first1, send(sum1, perm=outward), columns, True)
    a1 = send(x1, perm=inward)
    d1 = send(after(y1, b1), perm=inward)
    early1 = early_rows(own_w, [x1, y1], b1)
    field2, x2, y2, high = meet(first2, send(sum2, perm=outward), columns, False)
    a2 = send(x2, perm=inward)
    d2 = send(after(y2, a2), perm=inward)
    early2 = early_rows(own_w, [x2, y2], b2)
    c1 = send(after(a1, early1), perm=across)
    e1 = send(d1, perm=across)
    half = b1.shape[1] // 2
    left, right = slice(0, half), slice(half, 2 * half)
    sum1 = end_sum(edge_w, x1, b1, c1, left)
    out1 = send(sum1, perm=outward)
    rum1 = end_sum(edge_w, y1, b1, e1, right)
    rut1 = send(after(rum1, out1), perm=outward)
    before = lax.ppermute(after(high, b2, d1), "tile", up)
    behind = lax.ppermute(after(low, b2, d1), "tile", down)
    base1, base2 = local([field1, field2], before, behind)
    c2 = send(a2, perm=across)
    e2 = send(after(d2, c2), perm=across)
    sum2 = end_sum(edge_w, after(x2, rum1, before, early2), b2, c2, left)
    out2 = send(after(sum2, rut1, out1), perm=outward)
    rum2 = end_sum(edge_w, after(y2, sum2, base1), b2, e2, right)
    first1 = late_rows(own_w, [a1, d1], [c1, e1], base1, early1)
    rut2 = send(after(rum2, out2), perm=outward)
    first2 = late_rows(own_w, [after(a2, sum2), d2], [c2, e2], base2, early2)
    return unpack([first1, first2], [out1, rut1, out2, rut2], rows)


def extended(block, width):
    count = lax.axis_size("tile")
    up = [(i, i + 1) for i in range(count - 1)]
    down = [(i + 1, i) for i in range(count - 1)]
    low = lax.ppermute(block[:, -width:], "tile", up)
    high = lax.ppermute(block[:, :width], "tile", down)
    return jnp.concatenate([low, block, high], axis=1)


def gathered(distribution, courant, relax_rate, scatter_weight, cell_flags):
    cx = courant[0][:, None, None]
    cy = courant[1][:, None, None]
    rate = relax_rate[:, None, None]
    flags = cell_flags.astype(f32)[None]
    weight = scatter_weight.astype(bf16)
    field = distribution
    for step in range(2):
        full = jnp.pad(extended(field, 2), ((0, 0), (0, 0), (2, 2)))
        centre = full[:, 2:-2, 2:-2]
        back_x = 1.5 * centre - 2.0 * full[:, 1:-3, 2:-2] + 0.5 * full[:, :-4, 2:-2]
        fwd_x = -1.5 * centre + 2.0 * full[:, 3:-1, 2:-2] - 0.5 * full[:, 4:, 2:-2]
        back_y = 1.5 * centre - 2.0 * full[:, 2:-2, 1:-3] + 0.5 * full[:, 2:-2, :-4]
        fwd_y = -1.5 * centre + 2.0 * full[:, 2:-2, 3:-1] - 0.5 * full[:, 2:-2, 4:]
        transport = (
            jnp.maximum(cx, 0.0) * back_x
            + jnp.minimum(cx, 0.0) * fwd_x
            + jnp.maximum(cy, 0.0) * back_y
            + jnp.minimum(cy, 0.0) * fwd_y
        )
        flat = field.astype(bf16).reshape(field.shape[0], -1)
        flat = lax.all_gather(flat, "mode", axis=0, tiled=True)
        gain = jnp.dot(weight, flat, preferred_element_type=f32).reshape(field.shape)
        field = field - transport + time_step * (gain - rate * field - wall_rate * flags * field)
    return field


def body(*args):
    if lax.axis_size("mode") == 4 and lax.axis_size("tile") == 8 and args[0].shape[1] % 4 == 0:
        return line_of_four(*args)
    return gathered(*args)


def solution(mesh):
    in_specs = (
        P("mode", "tile", None),
        P(None, "mode"),
        P("mode"),
        P("mode", None),
        P("tile", None),
    )
    out_specs = P("mode", "tile", None)
    return jax.shard_map(body, mesh=mesh, in_specs=in_specs, out_specs=out_specs, check_vma=False)
```

```python
import functools

import jax
import jax.numpy as jnp
from jax import lax
from jax.experimental import pallas as pl
from jax.experimental.pallas import tpu as pltpu
from jax.sharding import PartitionSpec as P

time_step = 0.25
wall_rate = 2.0
bf16 = jnp.bfloat16
f32 = jnp.float32


def small(limit):
    return dict(
        cost_estimate=pl.CostEstimate(flops=1000, bytes_accessed=1000, transcendentals=0),
        compiler_params=pltpu.CompilerParams(vmem_limit_bytes=limit * 2**20),
    )


def pack_kernel(blocks, field_ref, one_ref, two_ref, low_ref, high_ref, held_ref, done_ref):
    modes, cells = one_ref.shape
    columns = field_ref.shape[1]
    half = cells // columns
    rows = 2 * half
    block = modes // blocks
    copies = []
    for i in range(blocks):
        at = pl.ds(i * block * rows, block * rows)
        copies.append(pltpu.make_async_copy(field_ref.at[at], held_ref.at[at], done_ref.at[i]))
        copies[i].start()
    for i in range(blocks):
        copies[i].wait()
        to = slice(i * block, (i + 1) * block)
        for r in range(rows):
            line = held_ref[pl.ds(i * block * rows + r, block, stride=rows), :]
            to_ref = one_ref if r < half else two_ref
            to_ref[to, r % half * columns:(r % half + 1) * columns] = line.astype(bf16)
            if r < 2:
                low_ref[to, r * columns:(r + 1) * columns] = line
            if r >= rows - 2:
                at = r - rows + 2
                high_ref[to, at * columns:(at + 1) * columns] = line


def pack(field):
    modes, rows, columns = field.shape
    blocks = 8
    shape = lambda count, kind: jax.ShapeDtypeStruct((modes, count * columns), kind)
    return pl.pallas_call(
        functools.partial(pack_kernel, blocks),
        in_specs=[pl.BlockSpec(memory_space=pl.ANY)],
        out_specs=[pl.BlockSpec(memory_space=pltpu.VMEM)] * 4,
        out_shape=[shape(rows // 2, bf16)] * 2 + [shape(2, f32)] * 2,
        scratch_shapes=[pltpu.VMEM((modes * rows, columns), f32), pltpu.SemaphoreType.DMA((blocks,))],
        name="pack",
        **small(46),
    )(field.reshape(modes * rows, columns))


def local_line(lines, r, params, flags):
    cx, cy, rate = params
    centre = lines(r)
    lane = lax.broadcasted_iota(jnp.int32, centre.shape, 1)
    columns = centre.shape[1]

    def moved(by):
        turned = pltpu.roll(centre, by % columns, 1)
        keep = lane >= by if by > 0 else lane < columns + by
        return jnp.where(keep, turned, 0.0)

    back_x = 1.5 * centre - 2.0 * lines(r - 1) + 0.5 * lines(r - 2)
    fwd_x = -1.5 * centre + 2.0 * lines(r + 1) - 0.5 * lines(r + 2)
    back_y = 1.5 * centre - 2.0 * moved(1) + 0.5 * moved(2)
    fwd_y = -1.5 * centre + 2.0 * moved(-1) - 0.5 * moved(-2)
    transport = (
        jnp.maximum(cx, 0.0) * back_x
        + jnp.minimum(cx, 0.0) * fwd_x
        + jnp.maximum(cy, 0.0) * back_y
        + jnp.minimum(cy, 0.0) * fwd_y
    )
    return centre - transport - time_step * (rate * centre + wall_rate * flags * centre)


def column(line):
    count = line.shape[1]
    at = lax.broadcasted_iota(jnp.int32, (count, count), 0)
    lane = lax.broadcasted_iota(jnp.int32, (count, count), 1)
    return jnp.sum(jnp.where(at == lane, line, 0.0), axis=1, keepdims=True)


def base_kernel(rows, modes, strided, *refs):
    *field_refs, before_ref, behind_ref, courant_ref, rate_ref, flags_ref, one_ref, two_ref = refs
    params = (column(courant_ref[0:1, :]), column(courant_ref[1:2, :]), column(rate_ref[...]))
    flags = flags_ref[...].astype(f32)
    columns = flags_ref.shape[1]
    half = rows // 2
    cut = lambda at: slice(at * columns, (at + 1) * columns)

    def lines(r):
        if r < 0:
            return before_ref[:, cut(r + 2)]
        if r >= rows:
            return behind_ref[:, cut(r - rows)]
        if strided:
            return field_refs[0][pl.ds(r, modes, stride=rows), :]
        return field_refs[r // half][:, cut(r % half)]

    for r in range(rows):
        to_ref = one_ref if r < half else two_ref
        to_ref[:, cut(r % half)] = local_line(lines, r, params, flags[r:r + 1, :])


def base(fields, before, behind, courant, rate, flags):
    rows, columns = flags.shape
    modes = before.shape[0]
    block = 128
    spec = lambda count: pl.BlockSpec((block, count * columns), lambda i: (i, 0))
    strided = len(fields) == 1
    if strided:
        field_specs = [pl.BlockSpec((block * rows, columns), lambda i: (i, 0))]
        fields = [fields[0].reshape(modes * rows, columns)]
    else:
        field_specs = [spec(rows // 2)] * 2
    per_mode = lambda count: pl.BlockSpec((count, block), lambda i: (0, i))
    return pl.pallas_call(
        functools.partial(base_kernel, rows, block, strided),
        grid=(modes // block,),
        in_specs=field_specs + [spec(2), spec(2), per_mode(2), per_mode(1), pl.BlockSpec((rows, columns), lambda i: (0, 0))],
        out_specs=[spec(rows // 2)] * 2,
        out_shape=[jax.ShapeDtypeStruct((modes, rows // 2 * columns), f32)] * 2,
        name="base",
        **small(12),
    )(*fields, before, behind, courant, rate.reshape(1, modes), flags)


def piece_kernel(w_ref, out_ref, held_ref, done_ref):
    share, kept = out_ref.shape
    at = pl.multiple_of(lax.axis_index("tile") * share, share)
    skipped = w_ref.shape[1] - kept
    left = pl.multiple_of(jnp.where(lax.axis_index("mode") == 0, skipped, 0), skipped)
    count = done_ref.shape[0]
    rows = share // count
    spans = [pl.ds(i * rows, rows) for i in range(count)]
    copies = [
        pltpu.make_async_copy(w_ref.at[pl.ds(at + i * rows, rows), pl.ds(left, kept)], held_ref.at[span], done_ref.at[i])
        for i, span in enumerate(spans)
    ]
    for copy in copies:
        copy.start()
    for copy, span in zip(copies, spans):
        copy.wait()
        out_ref[span, :] = held_ref[span, :].astype(bf16)


def piece_of(weights, count):
    modes, depth = weights.shape
    shape = (modes // count, depth - modes)
    return pl.pallas_call(
        piece_kernel,
        in_specs=[pl.BlockSpec(memory_space=pl.ANY)],
        out_specs=pl.BlockSpec(memory_space=pltpu.VMEM),
        out_shape=jax.ShapeDtypeStruct(shape, bf16),
        scratch_shapes=[pltpu.VMEM(shape, f32), pltpu.SemaphoreType.DMA((4,))],
        name="piece",
        **small(56),
    )(weights)


def meet_kernel(low, first_ref, sum_ref, field_ref, one_ref, two_ref, side_ref):
    block = 128
    half = one_ref.shape[1]
    side = side_ref.shape[1]

    def step(i, _):
        at = pl.ds(pl.multiple_of(i * block, block), block)
        line = first_ref[at, :] + time_step * sum_ref[at, :].astype(f32)
        field_ref[at, :] = line
        rounded = line.astype(bf16)
        one_ref[at, :] = rounded[:, :half]
        two_ref[at, :] = rounded[:, half:]
        side_ref[at, :] = line[:, :side] if low else line[:, line.shape[1] - side:]
        return 0

    lax.fori_loop(0, first_ref.shape[0] // block, step, 0)


def meet(first, total, columns, low):
    modes, cells = first.shape
    vmem = pl.BlockSpec(memory_space=pltpu.VMEM)
    return pl.pallas_call(
        functools.partial(meet_kernel, low),
        in_specs=[vmem] * 2,
        out_specs=[vmem] * 4,
        out_shape=[
            jax.ShapeDtypeStruct((modes, cells), f32),
            jax.ShapeDtypeStruct((modes, cells // 2), bf16),
            jax.ShapeDtypeStruct((modes, cells // 2), bf16),
            jax.ShapeDtypeStruct((modes, 2 * columns), f32),
        ],
        name="meet",
        **small(12),
    )(first, total)


def cast_kernel(w_ref, out_ref):
    block = w_ref.shape[0]
    out_ref[pl.ds(pl.multiple_of(pl.program_id(0) * block, block), block), :] = w_ref[...].astype(bf16)


def cast(weights):
    block = 128
    return pl.pallas_call(
        cast_kernel,
        grid=(weights.shape[0] // block,),
        in_specs=[pl.BlockSpec((block, weights.shape[1]), lambda i: (i, 0))],
        out_specs=pl.BlockSpec(memory_space=pltpu.VMEM),
        out_shape=jax.ShapeDtypeStruct(weights.shape, bf16),
        name="cast",
        **small(36),
    )(weights)


def product(w_ref, span, parts, ours):
    plane = lax.axis_index("mode")
    beside = plane + 1 - 2 * lax.rem(plane, 2)
    owner = {0: plane, 1: beside, 2: 3 - plane, 3: 3 - beside}
    if not ours:
        skipped = jnp.where(plane < 2, 1, 0)
        owner = {j: jnp.clip(of - skipped, 0, 2) for j, of in owner.items()}
    total = None
    for j, pieces in parts.items():
        depth = pieces[0].shape[0]
        at = pl.multiple_of(owner[j] * depth, depth)
        weights = w_ref[span, pl.ds(at, depth)]
        terms = [jnp.dot(weights, piece[...], preferred_element_type=f32) for piece in pieces]
        term = terms[0] if len(terms) == 1 else jnp.concatenate(terms, axis=1)
        total = term if total is None else total + term
    return total


def parts_of(counts, refs):
    refs = iter(refs)
    return {j: [next(refs) for _ in range(count)] for j, count in counts.items()}


def own_kernel(counts, w_ref, *refs):
    *part_refs, base_ref, first_ref, rounded_ref = refs
    parts = parts_of(counts, part_refs)
    half = w_ref.shape[0] // 2
    for span in (slice(0, half), slice(half, 2 * half)):
        line = base_ref[span, :] + time_step * product(w_ref, span, parts, True)
        first_ref[span, :] = line
        rounded_ref[span, :] = line.astype(bf16)


def sum_kernel(counts, cut, this_ref, other_ref, *refs):
    *part_refs, sum_ref = refs
    parts = parts_of(counts, part_refs)
    if cut is not None:
        parts[2] = [parts[2][0].at[:, cut]]
    share = this_ref.shape[0] // 4
    x, y, core = place()
    for w_ref, of_core in ((this_ref, core), (other_ref, 1 - core)):
        total = product(w_ref, slice(None), parts, False).astype(bf16)
        for k, (of_x, of_y) in enumerate(((x, y), (1 - x, y), (x, 1 - y), (1 - x, 1 - y))):
            at = pl.multiple_of((4 * of_y + 2 * of_x + of_core) * share, share)
            sum_ref[pl.ds(at, share), :] = total[k * share:(k + 1) * share]


def place():
    tile = lax.axis_index("tile")
    return lax.rem(tile // 2, 2), tile // 4, lax.rem(tile, 2)


def gains(kernel, arrays, shape, kinds):
    vmem = pl.BlockSpec(memory_space=pltpu.VMEM)
    return pl.pallas_call(
        kernel,
        in_specs=[vmem] * len(arrays),
        out_specs=[vmem] * len(kinds),
        out_shape=[jax.ShapeDtypeStruct(shape, kind) for kind in kinds],
        name=kernel.func.__name__,
        **small(12),
    )(*arrays)


def own_rows(weights, x, a, b, c, based):
    parts = {0: x, 1: a, 2: b, 3: c}
    kernel = functools.partial(own_kernel, {j: len(part) for j, part in parts.items()})
    return gains(kernel, (weights, *x, *a, *b, *c, based), based.shape, (f32, bf16))


def end_sum(weights, x, b, c, cut=None):
    kernel = functools.partial(sum_kernel, {0: 1, 2: 1, 3: 1}, cut)
    return gains(kernel, (*weights, x, b, c), x.shape, (bf16,))[0]


def stack_kernel(*refs):
    out_ref = refs[-1]
    share = refs[0].shape[0]
    for k, ref in enumerate(refs[:-1]):
        out_ref[k * share:(k + 1) * share, :] = ref[...]


def stack(*pieces):
    share, depth = pieces[0].shape
    vmem = pl.BlockSpec(memory_space=pltpu.VMEM)
    return pl.pallas_call(
        stack_kernel,
        in_specs=[vmem] * len(pieces),
        out_specs=vmem,
        out_shape=jax.ShapeDtypeStruct((len(pieces) * share, depth), bf16),
        name="stack",
        **small(12),
    )(*pieces)


def unpack_kernel(rows, modes, *refs):
    *sum_refs, out_ref = refs[2:]
    columns = out_ref.shape[1]
    half, quarter = rows // 2, rows // 4
    for r in range(rows):
        at = slice(r % half * columns, (r % half + 1) * columns)
        of = slice(r % quarter * columns, (r % quarter + 1) * columns)
        line = refs[r // half][:, at] + time_step * sum_refs[r // quarter][:, of].astype(f32)
        out_ref[pl.ds(r, modes, stride=rows), :] = line


def unpack(firsts, sums, rows):
    modes, cells = firsts[0].shape
    columns = 2 * cells // rows
    block = 256
    spec = lambda count: pl.BlockSpec((block, count), lambda i: (i, 0))
    flat = pl.pallas_call(
        functools.partial(unpack_kernel, rows, block),
        grid=(modes // block,),
        in_specs=[spec(cells)] * 2 + [spec(cells // 2)] * 4,
        out_specs=pl.BlockSpec((block * rows, columns), lambda i: (i, 0)),
        out_shape=jax.ShapeDtypeStruct((modes * rows, columns), f32),
        name="unpack",
        **small(12),
    )(*firsts, *sums)
    return flat.reshape(modes, rows, columns)


inward = [(0, 1), (3, 2)]
outward = [(1, 0), (2, 3)]
across = [(1, 2), (2, 1)]


def line_of_four(distribution, courant, relax_rate, scatter_weight, cell_flags):
    modes, rows, columns = distribution.shape
    count = lax.axis_size("tile")
    up = [(i, i + 1) for i in range(count - 1)]
    down = [(i + 1, i) for i in range(count - 1)]
    send = functools.partial(lax.ppermute, axis_name="mode")
    after = lambda value, *earlier: lax.optimization_barrier((value, *earlier))[0]
    local = functools.partial(base, courant=courant, rate=relax_rate, flags=cell_flags)
    by = lambda value, bits: lax.ppermute(value, "tile", [(i, i ^ bits) for i in range(count)])

    piece = piece_of(scatter_weight, count)
    x1, x2, low, high = pack(distribution)
    piece = send(piece, perm=inward)
    b1 = send(x1, perm=across)
    b2 = send(after(x2, b1), perm=across)
    before = lax.ppermute(high, "tile", up)
    behind = lax.ppermute(low, "tile", down)
    a1 = send(x1, perm=inward)
    own_w = cast(after(scatter_weight, x1))
    base1, base2 = local([distribution], before, behind)
    from_piece = after(piece, own_w)
    px, py, pd = by(from_piece, 2), by(from_piece, 4), by(from_piece, 6)
    a2 = send(after(x2, a1, pd), perm=inward)
    c1 = send(after(a1, base1), perm=across)
    this = stack(after(piece, b2), px, py, pd)
    c2 = send(after(a2, this, pd), perm=across)
    edge_w = (this, by(after(this, a2, c1), 1))
    first1, own1 = own_rows(own_w, [x1], [a1], [b1], [c1], base1)
    sum1 = end_sum(edge_w, after(x1, own1), b1, c1)
    sum2 = end_sum(edge_w, x2, b2, c2)
    first2, own2 = own_rows(own_w, [after(x2, sum2)], [a2], [b2], [c2], base2)

    b1 = send(own1, perm=across)
    b2 = send(own2, perm=across)
    field1, x1, y1, low = meet(first1, send(sum1, perm=outward), columns, True)
    a1 = send(x1, perm=inward)
    d1 = send(after(y1, b1), perm=inward)
    field2, x2, y2, high = meet(first2, send(sum2, perm=outward), columns, False)
    a2 = send(x2, perm=inward)
    d2 = send(after(y2, a2), perm=inward)
    c1 = send(a1, perm=across)
    e1 = send(d1, perm=across)
    half = b1.shape[1] // 2
    left, right = slice(0, half), slice(half, 2 * half)
    sum1 = end_sum(edge_w, x1, b1, c1, left)
    out1 = send(sum1, perm=outward)
    rum1 = end_sum(edge_w, y1, b1, e1, right)
    rut1 = send(after(rum1, out1), perm=outward)
    before = lax.ppermute(after(high, b2, d1), "tile", up)
    behind = lax.ppermute(after(low, b2, d1), "tile", down)
    base1, base2 = local([field1, field2], before, behind)
    c2 = send(a2, perm=across)
    e2 = send(after(d2, c2), perm=across)
    sum2 = end_sum(edge_w, after(x2, rum1, before), b2, c2, left)
    out2 = send(after(sum2, rut1, out1), perm=outward)
    rum2 = end_sum(edge_w, after(y2, sum2, base1), b2, e2, right)
    first1, _ = own_rows(own_w, [x1, y1], [a1, d1], [b1], [c1, e1], base1)
    rut2 = send(after(rum2, out2), perm=outward)
    first2, _ = own_rows(own_w, [after(x2, sum2), y2], [a2, d2], [b2], [c2, e2], base2)
    return unpack([first1, first2], [out1, rut1, out2, rut2], rows)


def extended(block, width):
    count = lax.axis_size("tile")
    up = [(i, i + 1) for i in range(count - 1)]
    down = [(i + 1, i) for i in range(count - 1)]
    low = lax.ppermute(block[:, -width:], "tile", up)
    high = lax.ppermute(block[:, :width], "tile", down)
    return jnp.concatenate([low, block, high], axis=1)


def gathered(distribution, courant, relax_rate, scatter_weight, cell_flags):
    cx = courant[0][:, None, None]
    cy = courant[1][:, None, None]
    rate = relax_rate[:, None, None]
    flags = cell_flags.astype(f32)[None]
    weight = scatter_weight.astype(bf16)
    field = distribution
    for step in range(2):
        full = jnp.pad(extended(field, 2), ((0, 0), (0, 0), (2, 2)))
        centre = full[:, 2:-2, 2:-2]
        back_x = 1.5 * centre - 2.0 * full[:, 1:-3, 2:-2] + 0.5 * full[:, :-4, 2:-2]
        fwd_x = -1.5 * centre + 2.0 * full[:, 3:-1, 2:-2] - 0.5 * full[:, 4:, 2:-2]
        back_y = 1.5 * centre - 2.0 * full[:, 2:-2, 1:-3] + 0.5 * full[:, 2:-2, :-4]
        fwd_y = -1.5 * centre + 2.0 * full[:, 2:-2, 3:-1] - 0.5 * full[:, 2:-2, 4:]
        transport = (
            jnp.maximum(cx, 0.0) * back_x
            + jnp.minimum(cx, 0.0) * fwd_x
            + jnp.maximum(cy, 0.0) * back_y
            + jnp.minimum(cy, 0.0) * fwd_y
        )
        flat = field.astype(bf16).reshape(field.shape[0], -1)
        flat = lax.all_gather(flat, "mode", axis=0, tiled=True)
        gain = jnp.dot(weight, flat, preferred_element_type=f32).reshape(field.shape)
        field = field - transport + time_step * (gain - rate * field - wall_rate * flags * field)
    return field


def body(*args):
    if lax.axis_size("mode") == 4 and lax.axis_size("tile") == 8 and args[0].shape[1] % 4 == 0:
        return line_of_four(*args)
    return gathered(*args)


def solution(mesh):
    in_specs = (
        P("mode", "tile", None),
        P(None, "mode"),
        P("mode"),
        P("mode", None),
        P("tile", None),
    )
    out_specs = P("mode", "tile", None)
    return jax.shard_map(body, mesh=mesh, in_specs=in_specs, out_specs=out_specs, check_vma=False)
```
